256 devices in a mesh: seq: 32 (over z, y), ch: 8 (over x, core).
Axes of the slice: x: 4, y: 4, z: 8, core: 2. Of those that a mesh axis runs over, the one named last changes fastest.
Arguments:
- tokens: bfloat16 [8192, 8192], P('seq', 'ch'), may hold values from -6 to 6
- w_in: bfloat16 [8, 1024, 3, 4096], P(None, 'seq', None, 'ch'), may hold values from -0.0625 to 0.0625
- taps: float32 [3, 3, 4096], P(None, None, 'ch'), may hold values from -3.5 to 3.5
- filt: float32 [8192, 4096], P('seq', 'ch'), may hold values from -0.0625 to 0.0625
- bias: float32 [4096], P('ch'), may hold values from -1 to 1
Outputs:
- gated: bfloat16 [8192, 4096], P('seq', 'ch')
The draws below stay inside these ranges and needn't reach their ends.
All inputs are finite; a program needn't handle non-finite values.
Results may differ from the reference program's by a relative error of at most 0.017.
Values may be sent and summed in bfloat16 or wider, within the bound.
A program may use at most 128 MiB of HBM per device.

```python
import jax
import jax.numpy as jnp

D = 8192
C = 4096
TOKENS = 8192
N_CH = 8


def block_scale(stream_key, extent, cuts, least, top_value):
    factor_of, own = 1.0, jax.random.fold_in(stream_key, 6)
    for dim, blocks in cuts:
        heights = jnp.exp(jax.random.uniform(jax.random.fold_in(own, dim), (blocks,), jnp.float32, least / len(cuts), top_value / len(cuts)))
        factor_of = factor_of * jnp.repeat(heights, extent[dim] // blocks).reshape([-1 if axis == dim else 1 for axis in range(len(extent))])
    return factor_of


def gaussian(own_key, dims, scale, bound, shards=(), kind=jnp.bfloat16):
    gain = block_scale(own_key, dims, shards, -0.22, 0.18) if shards else 1.0
    result = jax.random.normal(own_key, dims, jnp.float32) * scale * gain
    return jnp.minimum(jnp.maximum(result, -bound), bound).astype(kind)


def setup_inputs(seed: int = 0) -> dict:
    streams_of = jax.random.split(jax.random.key(seed), 6)
    tokens = gaussian(streams_of[0], (TOKENS, D), 1.0, 6.0, ((0, 32), (1, 8)))
    w_in = gaussian(streams_of[1], (N_CH, D // N_CH, 3, C), D ** -0.5, 0.0625, ((1, 32), (3, 8)))
    taps = gaussian(streams_of[2], (3, 3, C), 3 ** -0.5, 3.5, ((2, 8),), jnp.float32)
    filt = gaussian(streams_of[3], (TOKENS, C), TOKENS ** -0.5, 0.0625, ((0, 32), (1, 8)), jnp.float32)
    bias = jnp.clip(jax.random.uniform(streams_of[4], (C,), jnp.float32, -1.0, 1.0) * block_scale(streams_of[4], (C,), ((0, 8),), -0.4, 0.0), -1.0, 1.0)
    return {"tokens": tokens, "w_in": w_in, "taps": taps, "filt": filt, "bias": bias}


def reference(tokens, w_in, taps, filt, bias):
    flat = w_in.reshape(D, 3 * C)
    proj = jnp.dot(tokens, flat, preferred_element_type=jnp.float32).astype(jnp.bfloat16)
    proj = proj.reshape(TOKENS, 3, C).astype(jnp.float32)
    padded = jnp.concatenate([jnp.zeros((2, 3, C), jnp.float32), proj], axis=0)
    short = taps[0] * padded[2:] + taps[1] * padded[1:-1] + taps[2] * padded[:-2]
    query = short[:, 0, :]
    signal = short[:, 1, :] * short[:, 2, :]
    length = 2 * TOKENS
    spec_signal = jnp.fft.rfft(signal, n=length, axis=0)
    spec_filt = jnp.fft.rfft(filt, n=length, axis=0)
    conv = jnp.fft.irfft(spec_signal * spec_filt, n=length, axis=0)[:TOKENS]
    long_out = conv + bias * signal
    return (query * long_out).astype(jnp.bfloat16)
```

```python
import functools

import jax
import jax.numpy as jnp
import ml_dtypes
import numpy as np
from jax import lax
from jax.experimental import pallas as pl
from jax.experimental.pallas import tpu as pltpu
from jax.sharding import PartitionSpec as P

MESH = pl.DeviceIdType.MESH
BF = jnp.bfloat16
F32 = jnp.float32

Z, Y, X = 8, 4, 4
ROWS = 256
FEAT = 1024
GROUP = Y * ROWS
CH = 128
CW = CH // Z
WR = 32
N1, N2 = 64, 128
POINTS = N1 * N2
THETA = 0.25
PIECE = (0, -1, 1, 2)


def split(value):
    high = value.astype(ml_dtypes.bfloat16)
    low = (value - high.astype(np.float64)).astype(ml_dtypes.bfloat16)
    return np.stack([high, low])


@functools.cache
def tables():
    k1 = np.arange(N1)[:, None] + THETA
    angle = 2 * np.pi * k1 * np.arange(N1)[None, :] / N1
    first = np.concatenate([np.cos(angle), -np.sin(angle)], axis=0)
    angle = 2 * np.pi * k1 * np.arange(N2)[None, :] / POINTS
    twiddle = np.stack([np.cos(angle), -np.sin(angle)]).astype(np.float32)
    angle = 2 * np.pi * (np.arange(N2)[:, None] * np.arange(N2)[None, :] % N2) / N2
    cos, sin = np.cos(angle), np.sin(angle)
    second = np.block([[cos, -sin], [sin, cos]])
    second_back = np.block([[cos, sin], [-sin, cos]])
    return (
        split(first),
        split(first.T / POINTS),
        twiddle,
        split(second),
        split(second_back),
    )


def dot(a, b):
    return jnp.dot(a, b, preferred_element_type=F32)


def halves(value):
    high = value.astype(BF)
    return high, (value - high.astype(F32)).astype(BF)


def kernel(
    tok_in, w_in, filt, taps, bias, first, first_back, twiddle, second, second_back,
    out,
    tok, wall, acc, proj, halo_out, halo_in, query, signal, sig_t, conv_t, gated,
    filt_t, filt_z, x_in, h_in, spread, stage, high, low, spec_h, y_out,
    send_sem, recv_sem, local_sem,
):
    seq, ch = lax.axis_index("seq"), lax.axis_index("ch")
    z, y, x, core = seq // Y, seq % Y, ch // 2, ch % 2
    numbers = {}

    def number(key):
        return numbers.setdefault(key, len(numbers))

    def device(dz=0, dy=0, dx=0, flip=False):
        to_seq = ((z + dz + Z) % Z) * Y + (y + dy + Y) % Y
        to_ch = ((x + dx + X) % X) * 2 + (1 - core if flip else core)
        return (to_seq, to_ch)

    def remote(key, src, dst, target):
        n = number(key)
        return pltpu.make_async_remote_copy(
            src_ref=src, dst_ref=dst, send_sem=send_sem.at[n], recv_sem=recv_sem.at[n],
            device_id=target, device_id_type=MESH,
        )

    sent = []

    def send(key, src, dst, target):
        copy = remote(key, src, dst, target)
        copy.start()
        sent.append(copy)

    def receive(key, dst):
        remote(key, dst, dst, device(flip=True)).wait_recv()

    def w_place(dz, p):
        return wall.at[(z + dz + Z) % Z, :, pl.ds(((y + PIECE[p] + Y) % Y) * WR, WR), :]

    def t_place(dy, dx, other=False, half=None):
        b = ((x + dx + X) % X) * 2 + (1 - core if other else core)
        start = ((y + dy + Y) % Y) * ROWS
        if half is None:
            return tok.at[b, pl.ds(start, ROWS), :]
        return tok.at[b, pl.ds(start + half * (ROWS // 2), ROWS // 2), :]

    def along(axis, step):
        on_x = (1 - core) if axis == 0 else core
        return step * (1 - on_x), step * on_x

    def shift(axis, step):
        dy, dx = along(axis, step)
        return device(dy=dy, dx=dx)

    own_tok = pltpu.make_async_copy(tok_in, t_place(0, 0), local_sem.at[0])
    own_w = pltpu.make_async_copy(w_in.at[y], w_place(0, 0), local_sem.at[1])
    own_tok.start()
    own_w.start()

    peers = [device(dz=d) for d in range(1, Z)] + [device(dy=d) for d in range(1, Y)]
    peers += [device(dx=1), device(dx=-1), device(flip=True)]
    barrier = pltpu.get_barrier_semaphore()
    for peer in peers:
        pl.semaphore_signal(barrier, inc=1, device_id=peer, device_id_type=MESH)
    pl.semaphore_wait(barrier, len(peers))

    own_w.wait()

    def z_send(d, p, right):
        step = 1 if right else -1
        place = w_place(-step * d, p)
        send(("z", right, d + 1, p), place, place, device(dz=step))

    for p in (1, 2, 3):
        to = -PIECE[p]
        send(
            ("wy", p),
            w_in.at[(y + to + Y) % Y],
            wall.at[z, :, pl.ds(y * WR, WR), :],
            device(dy=to),
        )
        if p == 1:
            z_send(0, 0, True)
            z_send(0, 0, False)

    own_tok.wait()

    OFFSET = (0, 0, 1, -1, 2)

    def block(ring, step, half=None):
        if ring == 0:
            dy, dx = along(0, step)
        else:
            ay, ax = along(0, OFFSET[ring])
            by, bx = along(1, step)
            dy, dx = ay + by, ax + bx
        return t_place(dy + Y, dx + X, half=half)

    def t_send(ring, right, half, d):
        step = 1 if right else -1
        place = block(ring, -step * d, half)
        send(("t", ring, right, half, d + 1), place, place, shift(0 if ring == 0 else 1, step))

    def to_sibling(ring, step):
        place = block(ring, step)
        send(("s", ring, step), place, place, device(flip=True))

    def begin(ring):
        t_send(ring, True, 0, 0)
        t_send(ring, False, 1, 0)
        t_send(ring, True, 1, 0)
        t_send(ring, False, 0, 0)

    def near_first(ring):
        receive(("t", ring, True, 0, 1), block(ring, -1, 0))
        t_send(ring, True, 0, 1)
        receive(("t", ring, False, 1, 1), block(ring, 1, 1))
        t_send(ring, False, 1, 1)

    def near_second(ring):
        receive(("t", ring, True, 1, 1), block(ring, -1, 1))
        receive(("t", ring, False, 0, 1), block(ring, 1, 0))
        to_sibling(ring, -1)
        to_sibling(ring, 1)

    def far(ring):
        receive(("t", ring, True, 0, 2), block(ring, 2, 0))
        receive(("t", ring, False, 1, 2), block(ring, 2, 1))
        to_sibling(ring, 2)

    begin(0)
    begin(1)
    to_sibling(0, 0)

    for i in range(2):
        for quarter in range(4):
            part = filt[i * N2:(i + 1) * N2, quarter * CH:(quarter + 1) * CH]
            filt_t[i, quarter * CH:(quarter + 1) * CH, :] = part.T.astype(BF)
    for d in range(1, Y):
        to = (y + d) % Y
        send(
            ("fy", d),
            filt_t.at[:, pl.ds(to * CH, CH), :],
            filt_z.at[pl.ds(2 * y, 2), :, :],
            device(dy=d),
        )
    filt_z[pl.ds(2 * y, 2), :, :] = filt_t[:, pl.ds(pl.multiple_of(y * CH, CH), CH), :]
    acc[...] = jnp.zeros_like(acc)

    for p in (1, 2, 3):
        receive(("wy", p), w_place(0, p))
        z_send(0, p, True)
        z_send(0, p, False)

    def across(name, src, dst):
        for d in range(1, Z):
            to = (z + d) % Z
            send(
                (name, d),
                src.at[:, pl.ds(to * CW, CW), :],
                dst.at[pl.ds(z * Z, Z), :, :],
                device(dz=d),
            )
        dst[pl.ds(z * Z, Z), :, :] = src[:, pl.ds(pl.multiple_of(z * CW, CW), CW), :]

    def across_wait(name, dst):
        for d in range(1, Z):
            receive((name, d), dst.at[pl.ds(((z - d + Z) % Z) * Z, Z), :, :])

    def transform(source):
        spread[...] = source[...].astype(F32).reshape(N1 * CW, N2)
        for c in range(0, CW, 2):
            both = jnp.concatenate(
                [spread[pl.ds(c + s, N1, stride=CW), :].astype(BF) for s in range(2)], axis=1
            )
            part = dot(first[0], both) + dot(first[1], both)
            for s in range(2):
                re, im = part[:N1, s * N2:(s + 1) * N2], part[N1:, s * N2:(s + 1) * N2]
                turned = jnp.concatenate(
                    [re * twiddle[0] - im * twiddle[1], re * twiddle[1] + im * twiddle[0]], axis=1
                )
                rows = pl.ds((c + s) * N1, N1)
                high[rows, :], low[rows, :] = halves(turned)
        product(second)

    def product(matrix):
        def rows_of(i, carry):
            rows = pl.ds(pl.multiple_of(i * 256, 256), 256)
            stage[rows, :] = dot(high[rows, :], matrix[0]) + (
                dot(low[rows, :], matrix[0]) + dot(high[rows, :], matrix[1])
            )
            return carry

        lax.fori_loop(0, CW * N1 // 256, rows_of, 0)

    def filter_across():
        for d in range(1, Y):
            receive(("fy", d), filt_z.at[pl.ds(2 * ((y - d + Y) % Y), 2), :, :])
        across("fz", filt_z, h_in)

    def filter_transform():
        across_wait("fz", h_in)
        transform(h_in)
        spec_h[...] = stage[...]

    def next_rings():
        begin(2)
        begin(3)

    def last_ring():
        begin(4)

    between = {
        0: [lambda: near_first(0), lambda: near_second(0), next_rings],
        1: [lambda: far(0), last_ring, lambda: near_first(1)],
        2: [lambda: near_second(1), lambda: far(1)],
        3: [lambda: near_first(2), lambda: near_second(2), filter_across],
        4: [lambda: far(2)],
        5: [lambda: near_first(3), lambda: near_second(3)],
        6: [lambda: far(3), filter_transform],
        7: [lambda: near_first(4)],
        8: [lambda: near_second(4)],
        9: [lambda: far(4)],
    }
    for d in range(1, 4):
        for p in range(4):
            for event in between.get((d - 1) * 4 + p, []):
                event()
            receive(("z", True, d, p), w_place(-d, p))
            if d < 3 or p < 2:
                z_send(d, p, True)
            receive(("z", False, d, p), w_place(d, p))
            if d < 3 or p >= 2:
                z_send(d, p, False)

    for ring in range(5):
        for step in ((0, -1, 1, 2) if ring == 0 else (-1, 1, 2)):
            if ring == 0:
                dy, dx = step * (1 - core), step * core
            else:
                dy = OFFSET[ring] * (1 - core) + step * core
                dx = OFFSET[ring] * core + step * (1 - core)
            receive(("s", ring, step), t_place(dy + Y, dx + X, other=True))

    def chunk(source, rows):
        left = jnp.concatenate(
            [
                tok[b, rows, pl.ds(pl.multiple_of(source * N2, N2), N2)]
                for b in range(2 * X)
            ],
            axis=1,
        )
        return dot(left, wall[source].reshape(FEAT, 3 * CH))

    def gather_sum(n, carry):
        source = (z + 5 + n // 4) % Z
        rows = pl.ds(pl.multiple_of((n % 4) * ROWS, ROWS), ROWS)
        acc[rows, :] += chunk(source, rows)
        return carry

    lax.fori_loop(0, 28, gather_sum, 0)
    for p in range(4):
        receive(("z", p < 2, 4, p), w_place(4, p))

    for part in (3, 0, 1, 2):
        rows = pl.ds(part * ROWS, ROWS)
        rounded = (acc[rows, :] + chunk((z + 4) % Z, rows)).astype(BF)
        proj[pl.ds(8 + part * ROWS, ROWS), :] = rounded.astype(F32)
        if part == 3:
            halo_out[...] = rounded[ROWS - 16:, :]
            send(("halo",), halo_out, halo_in, device(dz=1))

    mine = pl.ds(pl.multiple_of(y * CH, CH), CH)

    def short(i, j):
        columns = slice(j * CH, (j + 1) * CH)
        return sum(
            taps[s, j:j + 1, mine] * proj[pl.ds(8 - s + i * N2, N2), columns] for s in range(3)
        )

    for i in reversed(range(8)):
        if i == 0:
            receive(("halo",), halo_in)
            before = halo_in[...].astype(F32)[8:, :]
            proj[:8, :] = jnp.where(z > 0, before, 0.0)
        rows = pl.ds(i * N2, N2)
        query[rows, :] = short(i, 0)
        value = short(i, 1) * short(i, 2)
        signal[rows, :] = value
        sig_t[i] = value.T.astype(BF)

    across("sz", sig_t, x_in)
    across_wait("sz", x_in)
    transform(x_in)

    def multiply(i, carry):
        rows = pl.ds(pl.multiple_of(i * N1, N1), N1)
        a_re, a_im = stage[rows, :N2], stage[rows, N2:]
        b_re, b_im = spec_h[rows, :N2], spec_h[rows, N2:]
        high[rows, :], low[rows, :] = halves(
            jnp.concatenate([a_re * b_re - a_im * b_im, a_re * b_im + a_im * b_re], axis=1)
        )
        return carry

    lax.fori_loop(0, CW, multiply, 0)
    product(second_back)
    for c in range(0, CW, 2):
        turned = []
        for s in range(2):
            rows = pl.ds((c + s) * N1, N1)
            re, im = stage[rows, :N2], stage[rows, N2:]
            turned.append(
                jnp.concatenate(
                    [re * twiddle[0] + im * twiddle[1], im * twiddle[0] - re * twiddle[1]], axis=0
                )
            )
        top, rest = halves(jnp.concatenate(turned, axis=1))
        part = dot(first_back[0], top) + (dot(first_back[0], rest) + dot(first_back[1], top))
        for s in range(2):
            spread[pl.ds(c + s, N1, stride=CW), :] = part[:, s * N2:(s + 1) * N2]
    y_out[...] = spread[...].astype(BF).reshape(N1, CW, N2)

    for d in range(1, Z):
        to = (z + d) % Z
        send(
            ("yz", d),
            y_out.at[pl.ds(to * Z, Z), :, :],
            conv_t.at[:, pl.ds(z * CW, CW), :],
            device(dz=d),
        )
    conv_t[:, pl.ds(pl.multiple_of(z * CW, CW), CW), :] = y_out[pl.ds(z * Z, Z), :, :]
    for d in range(1, Z):
        receive(("yz", d), conv_t.at[:, pl.ds(((z - d + Z) % Z) * CW, CW), :])

    for d in (2, 1, 3, 0):
        to = (y + d) % Y
        for i in range(2):
            rows = pl.ds(pl.multiple_of(to * ROWS + i * N2, N2), N2)
            conv = conv_t[2 * to + i].astype(F32).T
            gated[rows, :] = (
                query[rows, :] * (conv + bias[:, mine] * signal[rows, :])
            ).astype(BF)
        rows = pl.ds(pl.multiple_of(to * ROWS, ROWS), ROWS)
        if d:
            send(("out", d), gated.at[rows, :], out.at[:, mine], device(dy=d))
        else:
            out[:, mine] = gated[rows, :]
    for d in range(1, Y):
        columns = pl.ds(pl.multiple_of(((y - d + Y) % Y) * CH, CH), CH)
        receive(("out", d), out.at[:, columns])
    for copy in sent:
        copy.wait_send()


COPIES = 3 + 28 + 30 + 16 + 3 + 7 + 7 + 1 + 7 + 3


def on_device(tokens, w_in, taps, filt, bias):
    w_parts = w_in.reshape(2 * X, WR, 3, Y, CH).transpose(3, 0, 1, 2, 4)
    w_parts = w_parts.reshape(Y, 2 * X, WR, 3 * CH)
    any_space = pl.BlockSpec(memory_space=pl.ANY)
    vmem = pl.BlockSpec(memory_space=pltpu.VMEM)
    scratch = [
        pltpu.VMEM((2 * X, GROUP, FEAT), BF),
        pltpu.VMEM((Z, 2 * X, Y * WR, 3 * CH), BF),
        pltpu.VMEM((GROUP, 3 * CH), F32),
        pltpu.VMEM((GROUP + 8, 3 * CH), F32),
        pltpu.VMEM((16, 3 * CH), BF),
        pltpu.VMEM((16, 3 * CH), BF),
        pltpu.VMEM((GROUP, CH), F32),
        pltpu.VMEM((GROUP, CH), F32),
        pltpu.VMEM((8, CH, N2), BF),
        pltpu.VMEM((8, CH, N2), BF),
        pltpu.VMEM((GROUP, CH), BF),
        pltpu.VMEM((2, Y * CH, N2), BF),
        pltpu.VMEM((8, CH, N2), BF),
        pltpu.VMEM((N1, CW, N2), BF),
        pltpu.VMEM((N1, CW, N2), BF),
        pltpu.VMEM((N1 * CW, N2), F32),
        pltpu.VMEM((CW * N1, 2 * N2), F32),
        pltpu.VMEM((CW * N1, 2 * N2), BF),
        pltpu.VMEM((CW * N1, 2 * N2), BF),
        pltpu.VMEM((CW * N1, 2 * N2), F32),
        pltpu.VMEM((N1, CW, N2), BF),
        pltpu.SemaphoreType.DMA((COPIES,)),
        pltpu.SemaphoreType.DMA((COPIES,)),
        pltpu.SemaphoreType.DMA((2,)),
    ]
    return pl.pallas_call(
        kernel,
        out_shape=jax.ShapeDtypeStruct((ROWS, Y * CH), BF),
        in_specs=[any_space, any_space] + [vmem] * 8,
        out_specs=vmem,
        scratch_shapes=scratch,
        compiler_params=pltpu.CompilerParams(
            collective_id=0, has_side_effects=True, vmem_limit_bytes=50 * 1024 * 1024
        ),
        name="layer",
    )(tokens, w_parts, filt, taps, bias[None, :], *(jnp.asarray(t) for t in tables()))


def solution(mesh):
    return jax.shard_map(
        on_device,
        mesh=mesh,
        in_specs=(
            P("seq", "ch"),
            P(None, "seq", None, "ch"),
            P(None, None, "ch"),
            P("seq", "ch"),
            P("ch"),
        ),
        out_specs=P("seq", "ch"),
        check_vma=False,
    )
```

```python
import functools

import jax
import jax.numpy as jnp
import ml_dtypes
import numpy as np
from jax import lax
from jax.experimental import pallas as pl
from jax.experimental.pallas import tpu as pltpu
from jax.sharding import PartitionSpec as P

MESH = pl.DeviceIdType.MESH
BF = jnp.bfloat16
F32 = jnp.float32

Z, Y, X = 8, 4, 4
ROWS = 256
FEAT = 1024
GROUP = Y * ROWS
CH = 128
PARTS = 2
CW = CH // Z // PARTS
WR = 32
N1, N2 = 64, 128
POINTS = N1 * N2
THETA = 0.25
FAR_FIRST = (4, 3, 5, 2, 6, 1, 7)
PIECE = (0, -1, 1, 2)


def split(value):
    high = value.astype(ml_dtypes.bfloat16)
    low = (value - high.astype(np.float64)).astype(ml_dtypes.bfloat16)
    return np.stack([high, low])


@functools.cache
def tables():
    k1 = np.arange(N1)[:, None] + THETA
    angle = 2 * np.pi * k1 * np.arange(N1)[None, :] / N1
    first = np.concatenate([np.cos(angle), -np.sin(angle)], axis=0)
    angle = 2 * np.pi * k1 * np.arange(N2)[None, :] / POINTS
    twiddle = np.stack([np.cos(angle), -np.sin(angle)]).astype(np.float32)
    angle = 2 * np.pi * (np.arange(N2)[:, None] * np.arange(N2)[None, :] % N2) / N2
    cos, sin = np.cos(angle), np.sin(angle)
    second = split(np.block([[cos, -sin], [sin, cos]]))
    second_back = split(np.block([[cos, sin], [-sin, cos]]))
    first_back = split(first.T / POINTS)
    return (
        np.concatenate(list(split(first)), axis=1),
        np.concatenate([first_back[0], first_back[0], first_back[1]], axis=1),
        twiddle,
        np.concatenate([second[0], second[0], second[1]], axis=0),
        np.concatenate([second_back[0], second_back[0], second_back[1]], axis=0),
    )


def dot(a, b):
    return jnp.dot(a, b, preferred_element_type=F32)


def halves(value):
    high = value.astype(BF)
    return high, (value - high.astype(F32)).astype(BF)


def by_channel(even, odd):
    turned = [value.T.reshape(CH // CW, CW, N2) for value in (even, odd)]
    return jnp.concatenate(turned, axis=1).astype(BF).reshape(PARTS, Z, 2 * CW, N2)


def kernel(
    tok_in, w_in, filt_in, taps_in, bias_in, first_in, first_back_in, twiddle_in, second_in,
    second_back_in, out,
    filt, taps, bias, first, first_back, twiddle, second, second_back, tok, wall, acc, proj, halo_out, halo_in, query, signal, sig_t, conv_t, gated,
    filt_t, filt_z, x_in, h_in, spread, stage, split_rows, spec_h, y_out,
    send_sem, recv_sem, local_sem,
):
    seq, ch = lax.axis_index("seq"), lax.axis_index("ch")
    z, y, x, core = seq // Y, seq % Y, ch // 2, ch % 2
    numbers = {}

    def number(key):
        return numbers.setdefault(key, len(numbers))

    def device(dz=0, dy=0, dx=0, flip=False):
        to_seq = ((z + dz + Z) % Z) * Y + (y + dy + Y) % Y
        to_ch = ((x + dx + X) % X) * 2 + (1 - core if flip else core)
        return (to_seq, to_ch)

    def remote(key, src, dst, target):
        n = number(key)
        return pltpu.make_async_remote_copy(
            src_ref=src, dst_ref=dst, send_sem=send_sem.at[n], recv_sem=recv_sem.at[n],
            device_id=target, device_id_type=MESH,
        )

    sent = []

    def send(key, src, dst, target):
        copy = remote(key, src, dst, target)
        copy.start()
        sent.append(copy)

    def receive(key, dst):
        remote(key, dst, dst, device(flip=True)).wait_recv()

    def w_place(dz, p):
        return wall.at[(z + dz + Z) % Z, :, pl.ds(((y + PIECE[p] + Y) % Y) * WR, WR), :]

    def t_place(dy, dx, other=False, half=None):
        b = ((x + dx + X) % X) * 2 + (1 - core if other else core)
        start = ((y + dy + Y) % Y) * ROWS
        if half is None:
            return tok.at[b, pl.ds(start, ROWS), :]
        return tok.at[b, pl.ds(start + half * (ROWS // 2), ROWS // 2), :]

    def along(axis, step):
        on_x = (1 - core) if axis == 0 else core
        return step * (1 - on_x), step * on_x

    def shift(axis, step):
        dy, dx = along(axis, step)
        return device(dy=dy, dx=dx)

    own_tok = pltpu.make_async_copy(tok_in, t_place(0, 0), local_sem.at[0])
    def w_columns(to, j):
        return w_in.at[j, :, :, pl.ds(to * CH, CH)]

    def w_home(j):
        return wall.at[z, :, pl.ds(y * WR, WR), pl.ds(j * CH, CH)]

    own_w = [pltpu.make_async_copy(w_columns(y, j), w_home(j), local_sem.at[1 + j]) for j in range(3)]
    pairs = [(filt_in, filt), (taps_in, taps), (bias_in, bias), (first_in, first), (first_back_in, first_back)]
    pairs += [(twiddle_in, twiddle), (second_in, second), (second_back_in, second_back)]
    own = [pltpu.make_async_copy(a, b, local_sem.at[4 + n]) for n, (a, b) in enumerate(pairs)]
    for copy in own[:1] + own_w + [own_tok] + own[1:]:
        copy.start()

    peers = [device(dz=d) for d in range(1, Z)] + [device(dy=d) for d in range(1, Y)]
    peers += [device(dx=1), device(dx=-1), device(flip=True)]
    barrier = pltpu.get_barrier_semaphore()
    for peer in peers:
        pl.semaphore_signal(barrier, inc=1, device_id=peer, device_id_type=MESH)

    own[0].wait()
    for quarter in range(Y):
        columns = slice(quarter * CH, (quarter + 1) * CH)
        filt_t[quarter] = by_channel(filt[:N2, columns], filt[N2:, columns])
    acc[...] = jnp.zeros_like(acc)

    pl.semaphore_wait(barrier, len(peers))

    for copy in own_w:
        copy.wait()

    def z_send(d, p, right):
        step = 1 if right else -1
        place = w_place(-step * d, p)
        send(("z", right, d + 1, p), place, place, device(dz=step))

    def w_send(p):
        to = -PIECE[p]
        for j in range(3):
            send(("wy", p, j), w_columns((y + to + Y) % Y, j), w_home(j), device(dy=to))

    z_send(0, 0, True)
    z_send(0, 0, False)
    w_send(1)
    w_send(2)
    own_tok.wait()
    for copy in own[1:]:
        copy.wait()

    OFFSET = (0, 0, 1, -1, 2)

    def block(ring, step, half=None):
        if ring == 0:
            dy, dx = along(0, step)
        else:
            ay, ax = along(0, OFFSET[ring])
            by, bx = along(1, step)
            dy, dx = ay + by, ax + bx
        return t_place(dy + Y, dx + X, half=half)

    def t_send(ring, right, half, d):
        step = 1 if right else -1
        place = block(ring, -step * d, half)
        send(("t", ring, right, half, d + 1), place, place, shift(0 if ring == 0 else 1, step))

    def to_sibling(ring, step):
        place = block(ring, step)
        send(("s", ring, step), place, place, device(flip=True))

    def begin(ring):
        t_send(ring, True, 0, 0)
        t_send(ring, False, 1, 0)
        t_send(ring, True, 1, 0)
        t_send(ring, False, 0, 0)

    def begin_a(ring):
        t_send(ring, True, 0, 0)
        t_send(ring, False, 1, 0)

    def begin_b(ring):
        t_send(ring, True, 1, 0)
        t_send(ring, False, 0, 0)

    def near_first(ring):
        receive(("t", ring, True, 0, 1), block(ring, -1, 0))
        t_send(ring, True, 0, 1)
        receive(("t", ring, False, 1, 1), block(ring, 1, 1))
        t_send(ring, False, 1, 1)

    def near_second(ring):
        receive(("t", ring, True, 1, 1), block(ring, -1, 1))
        receive(("t", ring, False, 0, 1), block(ring, 1, 0))
        to_sibling(ring, -1)
        to_sibling(ring, 1)

    def far(ring):
        receive(("t", ring, True, 0, 2), block(ring, 2, 0))
        receive(("t", ring, False, 1, 2), block(ring, 2, 1))
        to_sibling(ring, 2)

    begin_a(0)
    w_send(3)
    begin_b(0)
    to_sibling(0, 0)

    def across(name, part, src, dst):
        for d in FAR_FIRST:
            send(
                (name, part, d),
                src.at[:, part, (z + d) % Z],
                dst.at[part, pl.ds(z * Y, Y)],
                device(dz=d),
            )
        dst[part, pl.ds(z * Y, Y)] = src[:, part, z]

    def across_wait(name, part, dst):
        for d in range(1, Z):
            receive((name, part, d), dst.at[part, pl.ds(((z - d + Z) % Z) * Y, Y)])

    def transform(source, part):
        spread[...] = source[part].astype(F32).reshape(N1 * CW, N2)
        together = jnp.concatenate(
            [spread[pl.ds(c, N1, stride=CW), :].astype(BF) for c in range(CW)], axis=1
        )
        values = dot(first[...], jnp.concatenate([together, together], axis=0))
        for c in range(CW):
            columns = slice(c * N2, (c + 1) * N2)
            re, im = values[:N1, columns], values[N1:, columns]
            turned = jnp.concatenate(
                [re * twiddle[0] - im * twiddle[1], re * twiddle[1] + im * twiddle[0]], axis=1
            )
            in_halves(c, turned)
        stage[...] = dot(split_rows[...], second[...])

    def in_halves(c, value):
        rows = pl.ds(c * N1, N1)
        top, rest = halves(value)
        split_rows[rows, :2 * N2] = top
        split_rows[rows, 2 * N2:4 * N2] = rest
        split_rows[rows, 4 * N2:] = top

    def filter_across():
        for d in range(1, Y):
            receive(("fy", d), filt_z.at[(y - d + Y) % Y])
        for part in range(PARTS):
            across("fz", part, filt_z, h_in)

    def filter_transform(part):
        across_wait("fz", part, h_in)
        transform(h_in, part)
        spec_h[part] = stage[...]

    def filter_send():
        for d in range(1, Y):
            send(("fy", d), filt_t.at[(y + d) % Y], filt_z.at[y], device(dy=d))
        filt_z[y] = filt_t[y]

    def w_next(p):
        for j in range(3):
            columns = pl.ds(j * CH, CH)
            rows = pl.ds(((y + PIECE[p] + Y) % Y) * WR, WR)
            receive(("wy", p, j), wall.at[z, :, rows, columns])
        z_send(0, p, True)
        z_send(0, p, False)

    def z_next(s):
        d, p = s // 4 + 1, s % 4
        receive(("z", True, d, p), w_place(-d, p))
        if d < 3 or p < 2:
            z_send(d, p, True)
        receive(("z", False, d, p), w_place(d, p))
        if d < 3 or p >= 2:
            z_send(d, p, False)

    def total(blocks, rows, offsets):
        left, right = [], []
        for offset in offsets:
            source = (z + offset + Z) % Z
            for b in blocks:
                left.append(tok[b, rows, pl.ds(pl.multiple_of(source * N2, N2), N2)])
                right.append(wall[source, b])
        return acc[rows, :] + dot(jnp.concatenate(left, axis=1), jnp.concatenate(right, axis=0))

    EARLY = (0, -1, 1, -2, 2)
    LATE = (-3, 3)

    def unit(ring):
        for step in (-1, 1, 2):
            dy = OFFSET[ring] * (1 - core) + step * core
            dx = OFFSET[ring] * core + step * (1 - core)
            receive(("s", ring, step), t_place(dy + Y, dx + X, other=True))
        step = OFFSET[ring]
        receive(("s", 0, step), t_place(step * (1 - core) + Y, step * core + X, other=True))
        column = (x + OFFSET[ring] + X) % X

        def rows_of(n, carry):
            rows = pl.ds(pl.multiple_of(n * ROWS, ROWS), ROWS)
            acc[rows, :] = total([column * 2], rows, EARLY)
            return carry

        lax.fori_loop(0, Y, rows_of, 0)
        rows = pl.ds(pl.multiple_of(((y + OFFSET[ring] + Y) % Y) * ROWS, ROWS), ROWS)
        acc[rows, :] = total([2 * b + 1 for b in range(X)], rows, EARLY)

    def late():
        def rows_of(n, carry):
            rows = pl.ds(pl.multiple_of(n * ROWS, ROWS), ROWS)
            acc[rows, :] = total(range(2 * X), rows, LATE)
            return carry

        lax.fori_loop(0, Y, rows_of, 0)

    order = [
        (w_next, 1), (w_next, 2), (near_first, 0), (begin, 1), (filter_send,), (w_next, 3), (z_next, 0),
        (near_second, 0), (begin, 2), (begin, 3), (near_first, 1), (z_next, 1), (near_second, 1), (z_next, 2),
        (z_next, 3), (near_first, 2), (far, 0), (begin, 4), (near_second, 2), (z_next, 4),
        (near_first, 3), (z_next, 5), (near_second, 3), (near_first, 4), (z_next, 6),
        (near_second, 4), (z_next, 7), (far, 1), (far, 2), (z_next, 8), (far, 3), (z_next, 9),
        (far, 4), (z_next, 10), (z_next, 11), (filter_across,), (unit, 1), (unit, 2), (unit, 3), (unit, 4),
        (late,),
    ]
    for event, *values in order:
        event(*values)

    for p in range(4):
        receive(("z", p < 2, 4, p), w_place(4, p))

    for n in (3, 0, 1, 2):
        rounded = total(range(2 * X), pl.ds(n * ROWS, ROWS), (4,)).astype(BF)
        proj[pl.ds(8 + n * ROWS, ROWS), :] = rounded.astype(F32)
        if n == 3:
            halo_out[...] = rounded[ROWS - 16:, :]
            send(("halo",), halo_out, halo_in, device(dz=1))

    mine = pl.ds(pl.multiple_of(y * CH, CH), CH)

    def short(start, j):
        columns = slice(j * CH, (j + 1) * CH)
        return sum(
            taps[s, j:j + 1, mine] * proj[pl.ds(8 - s + start, N2), columns] for s in range(3)
        )

    for n in (1, 2, 3, 0):
        if n == 0:
            receive(("halo",), halo_in)
            before = halo_in[...].astype(F32)[8:, :]
            proj[:8, :] = jnp.where(z > 0, before, 0.0)
        values = []
        for start in (n * ROWS, n * ROWS + N2):
            rows = pl.ds(start, N2)
            query[rows, :] = short(start, 0)
            values.append(short(start, 1) * short(start, 2))
            signal[rows, :] = values[-1]
        sig_t[n] = by_channel(*values)

    for part in range(PARTS):
        across("sz", part, sig_t, x_in)
    for part in range(PARTS):
        filter_transform(part)

    for part in range(PARTS):
        across_wait("sz", part, x_in)
        transform(x_in, part)
        for c in range(CW):
            rows = pl.ds(c * N1, N1)
            a_re, a_im = stage[rows, :N2], stage[rows, N2:]
            b_re, b_im = spec_h[part, rows, :N2], spec_h[part, rows, N2:]
            in_halves(
                c, jnp.concatenate([a_re * b_re - a_im * b_im, a_re * b_im + a_im * b_re], axis=1)
            )
        stage[...] = dot(split_rows[...], second_back[...])
        turned = []
        for c in range(CW):
            rows = pl.ds(c * N1, N1)
            re, im = stage[rows, :N2], stage[rows, N2:]
            turned.append(
                jnp.concatenate(
                    [re * twiddle[0] + im * twiddle[1], im * twiddle[0] - re * twiddle[1]], axis=0
                )
            )
        top, rest = halves(jnp.concatenate(turned, axis=1))
        values = dot(first_back[...], jnp.concatenate([top, rest, top], axis=0))
        for c in range(CW):
            spread[pl.ds(c, N1, stride=CW), :] = values[:, c * N2:(c + 1) * N2]
        y_out[part] = spread[...].astype(BF).reshape(Z * Y, 2 * CW, N2)
        for d in FAR_FIRST:
            send(
                ("yz", part, d),
                y_out.at[part, pl.ds(((z + d) % Z) * Y, Y)],
                conv_t.at[:, part, z],
                device(dz=d),
            )
        conv_t[:, part, z] = y_out[part, pl.ds(z * Y, Y)]
    for part in range(PARTS):
        for d in range(1, Z):
            receive(("yz", part, d), conv_t.at[:, part, (z - d + Z) % Z])

    for d in (2, 1, 3, 0):
        to = (y + d) % Y
        conv = conv_t[to].astype(F32).reshape(PARTS * Z, 2, CW, N2)
        for i in range(2):
            rows = pl.ds(pl.multiple_of(to * ROWS + i * N2, N2), N2)
            long = conv[:, i].reshape(CH, N2).T + bias[:, mine] * signal[rows, :]
            gated[rows, :] = (query[rows, :] * long).astype(BF)
        rows = pl.ds(pl.multiple_of(to * ROWS, ROWS), ROWS)
        if d:
            send(("out", d), gated.at[rows, :], out.at[:, mine], device(dy=d))
        else:
            out[:, mine] = gated[rows, :]
    for d in range(1, Y):
        columns = pl.ds(pl.multiple_of(((y - d + Y) % Y) * CH, CH), CH)
        receive(("out", d), out.at[:, columns])
    for copy in sent:
        copy.wait_send()


COPIES = 9 + 28 + 30 + 16 + 3 + 1 + 3 * 7 * PARTS + 3


def on_device(tokens, w_in, taps, filt, bias):
    w_parts = w_in.transpose(2, 0, 1, 3)
    any_space = pl.BlockSpec(memory_space=pl.ANY)
    vmem = pl.BlockSpec(memory_space=pltpu.VMEM)
    scratch = [
        pltpu.VMEM((ROWS, Y * CH), F32),
        pltpu.VMEM((3, 3, Y * CH), F32),
        pltpu.VMEM((1, Y * CH), F32),
        *(pltpu.VMEM(t.shape, t.dtype) for t in tables()),
        pltpu.VMEM((2 * X, GROUP, FEAT), BF),
        pltpu.VMEM((Z, 2 * X, Y * WR, 3 * CH), BF),
        pltpu.VMEM((GROUP, 3 * CH), F32),
        pltpu.VMEM((GROUP + 8, 3 * CH), F32),
        pltpu.VMEM((16, 3 * CH), BF),
        pltpu.VMEM((16, 3 * CH), BF),
        pltpu.VMEM((GROUP, CH), F32),
        pltpu.VMEM((GROUP, CH), F32),
        pltpu.VMEM((Y, PARTS, Z, 2 * CW, N2), BF),
        pltpu.VMEM((Y, PARTS, Z, 2 * CW, N2), BF),
        pltpu.VMEM((GROUP, CH), BF),
        pltpu.VMEM((Y, PARTS, Z, 2 * CW, N2), BF),
        pltpu.VMEM((Y, PARTS, Z, 2 * CW, N2), BF),
        pltpu.VMEM((PARTS, Z * Y, 2 * CW, N2), BF),
        pltpu.VMEM((PARTS, Z * Y, 2 * CW, N2), BF),
        pltpu.VMEM((N1 * CW, N2), F32),
        pltpu.VMEM((CW * N1, 2 * N2), F32),
        pltpu.VMEM((CW * N1, 6 * N2), BF),
        pltpu.VMEM((PARTS, CW * N1, 2 * N2), F32),
        pltpu.VMEM((PARTS, Z * Y, 2 * CW, N2), BF),
        pltpu.SemaphoreType.DMA((COPIES,)),
        pltpu.SemaphoreType.DMA((COPIES,)),
        pltpu.SemaphoreType.DMA((12,)),
    ]
    return pl.pallas_call(
        kernel,
        out_shape=jax.ShapeDtypeStruct((ROWS, Y * CH), BF),
        in_specs=[any_space] * 10,
        out_specs=vmem,
        scratch_shapes=scratch,
        compiler_params=pltpu.CompilerParams(
            collective_id=0, has_side_effects=True, vmem_limit_bytes=60 * 1024 * 1024
        ),
        name="layer",
    )(tokens, w_parts, filt, taps, bias[None, :], *(jnp.asarray(t) for t in tables()))


def solution(mesh):
    return jax.shard_map(
        on_device,
        mesh=mesh,
        in_specs=(
            P("seq", "ch"),
            P(None, "seq", None, "ch"),
            P(None, None, "ch"),
            P("seq", "ch"),
            P("ch"),
        ),
        out_specs=P("seq", "ch"),
        check_vma=False,
    )
```

```python
import functools

import jax
import jax.numpy as jnp
import ml_dtypes
import numpy as np
from jax import lax
from jax.experimental import pallas as pl
from jax.experimental.pallas import tpu as pltpu
from jax.sharding import PartitionSpec as P

MESH = pl.DeviceIdType.MESH
BF = jnp.bfloat16
F32 = jnp.float32

Z, Y, X = 8, 4, 4
ROWS = 256
FEAT = 1024
GROUP = Y * ROWS
CH = 128
PARTS = 2
CW = CH // Z // PARTS
WR = 32
N1, N2 = 64, 128
POINTS = N1 * N2
THETA = 0.25
FAR_FIRST = (4, 3, 5, 2, 6, 1, 7)
PIECE = (0, -1, 1, 2)


def split(value):
    high = value.astype(ml_dtypes.bfloat16)
    low = (value - high.astype(np.float64)).astype(ml_dtypes.bfloat16)
    return np.stack([high, low])


@functools.cache
def tables():
    k1 = np.arange(N1)[:, None] + THETA
    angle = 2 * np.pi * k1 * np.arange(N1)[None, :] / N1
    first = np.concatenate([np.cos(angle), -np.sin(angle)], axis=0)
    angle = 2 * np.pi * k1 * np.arange(N2)[None, :] / POINTS
    twiddle = np.stack([np.cos(angle), -np.sin(angle)]).astype(np.float32)
    angle = 2 * np.pi * (np.arange(N2)[:, None] * np.arange(N2)[None, :] % N2) / N2
    cos, sin = np.cos(angle), np.sin(angle)
    second = split(np.block([[cos, -sin], [sin, cos]]))
    second_back = split(np.block([[cos, sin], [-sin, cos]]))
    first_back = split(first.T / POINTS)
    return (
        np.concatenate(list(split(first)), axis=1),
        np.concatenate([first_back[0], first_back[0], first_back[1]], axis=1),
        twiddle,
        np.concatenate([second[0], second[0], second[1]], axis=0),
        np.concatenate([second_back[0], second_back[0], second_back[1]], axis=0),
    )


def dot(a, b):
    return jnp.dot(a, b, preferred_element_type=F32)


def halves(value):
    high = value.astype(BF)
    return high, (value - high.astype(F32)).astype(BF)


def by_channel(even, odd):
    turned = [value.T.reshape(CH // CW, CW, N2) for value in (even, odd)]
    return jnp.concatenate(turned, axis=1).astype(BF).reshape(PARTS, Z, 2 * CW, N2)


def kernel(
    tok_in, w_in, filt_in, taps_in, bias_in, first_in, first_back_in, twiddle_in, second_in,
    second_back_in, out,
    filt, taps, bias, first, first_back, twiddle, second, second_back, tok, wall, acc, proj, halo_out, halo_in, share_out, share_in, sig_t, conv_in,
    filt_t, filt_z, x_in, h_in, spread, stage, split_rows, spec_h, y_out,
    send_sem, recv_sem, local_sem,
):
    seq, ch = lax.axis_index("seq"), lax.axis_index("ch")
    z, y, x, core = seq // Y, seq % Y, ch // 2, ch % 2
    numbers = {}

    def number(key):
        return numbers.setdefault(key, len(numbers))

    def device(dz=0, dy=0, dx=0, flip=False):
        to_seq = ((z + dz + Z) % Z) * Y + (y + dy + Y) % Y
        to_ch = ((x + dx + X) % X) * 2 + (1 - core if flip else core)
        return (to_seq, to_ch)

    def remote(key, src, dst, target):
        n = number(key)
        return pltpu.make_async_remote_copy(
            src_ref=src, dst_ref=dst, send_sem=send_sem.at[n], recv_sem=recv_sem.at[n],
            device_id=target, device_id_type=MESH,
        )

    sent = []

    def send(key, src, dst, target):
        copy = remote(key, src, dst, target)
        copy.start()
        sent.append(copy)

    def receive(key, dst):
        remote(key, dst, dst, device(flip=True)).wait_recv()

    def w_place(dz, p):
        return wall.at[(z + dz + Z) % Z, :, pl.ds(((y + PIECE[p] + Y) % Y) * WR, WR), :]

    def t_place(dy, dx, other=False, half=None):
        b = ((x + dx + X) % X) * 2 + (1 - core if other else core)
        start = ((y + dy + Y) % Y) * ROWS
        if half is None:
            return tok.at[b, pl.ds(start, ROWS), :]
        return tok.at[b, pl.ds(start + half * (ROWS // 2), ROWS // 2), :]

    def along(axis, step):
        on_x = (1 - core) if axis == 0 else core
        return step * (1 - on_x), step * on_x

    def shift(axis, step):
        dy, dx = along(axis, step)
        return device(dy=dy, dx=dx)

    own_tok = pltpu.make_async_copy(tok_in, t_place(0, 0), local_sem.at[0])
    def w_columns(to, j):
        return w_in.at[:, j, :, pl.ds(to * CH, CH)]

    def w_home(j):
        return wall.at[z, :, pl.ds(y * WR, WR), pl.ds(j * CH, CH)]

    own_w = [pltpu.make_async_copy(w_columns(y, j), w_home(j), local_sem.at[1 + j]) for j in range(3)]
    pairs = [(filt_in, filt), (taps_in, taps), (bias_in, bias), (first_in, first), (first_back_in, first_back)]
    pairs += [(twiddle_in, twiddle), (second_in, second), (second_back_in, second_back)]
    own = [pltpu.make_async_copy(a, b, local_sem.at[4 + n]) for n, (a, b) in enumerate(pairs)]
    for copy in own[:1] + own_w + [own_tok] + own[1:]:
        copy.start()

    peers = [device(dz=dz, dy=dy) for dz in range(Z) for dy in range(Y) if dz or dy]
    peers += [device(dx=1), device(dx=-1), device(flip=True)]
    barrier = pltpu.get_barrier_semaphore()
    for peer in peers:
        pl.semaphore_signal(barrier, inc=1, device_id=peer, device_id_type=MESH)

    own[0].wait()
    for quarter in range(Y):
        columns = slice(quarter * CH, (quarter + 1) * CH)
        filt_t[:, :, quarter] = by_channel(filt[:N2, columns], filt[N2:, columns])
    acc[...] = jnp.zeros_like(acc)

    pl.semaphore_wait(barrier, len(peers))

    for copy in own_w:
        copy.wait()

    def z_send(d, p, right):
        step = 1 if right else -1
        place = w_place(-step * d, p)
        send(("z", right, d + 1, p), place, place, device(dz=step))

    def w_send(p):
        to = -PIECE[p]
        for j in range(3):
            send(("wy", p, j), w_columns((y + to + Y) % Y, j), w_home(j), device(dy=to))

    z_send(0, 0, True)
    z_send(0, 0, False)
    w_send(1)
    w_send(2)
    for d in FAR_FIRST:
        send(("fz", 0, d), filt_t.at[0, (z + d) % Z], filt_z.at[0, z], device(dz=d))
    filt_z[0, z] = filt_t[0, z]
    own_tok.wait()
    for copy in own[1:]:
        copy.wait()

    OFFSET = (0, 0, 1, -1, 2)

    def block(ring, step, half=None):
        if ring == 0:
            dy, dx = along(0, step)
        else:
            ay, ax = along(0, OFFSET[ring])
            by, bx = along(1, step)
            dy, dx = ay + by, ax + bx
        return t_place(dy + Y, dx + X, half=half)

    def t_send(ring, right, half, d):
        step = 1 if right else -1
        place = block(ring, -step * d, half)
        send(("t", ring, right, half, d + 1), place, place, shift(0 if ring == 0 else 1, step))

    def to_sibling(ring, step):
        place = block(ring, step)
        send(("s", ring, step), place, place, device(flip=True))

    def begin(ring):
        t_send(ring, True, 0, 0)
        t_send(ring, False, 1, 0)
        t_send(ring, True, 1, 0)
        t_send(ring, False, 0, 0)

    def begin_a(ring):
        t_send(ring, True, 0, 0)
        t_send(ring, False, 1, 0)

    def begin_b(ring):
        t_send(ring, True, 1, 0)
        t_send(ring, False, 0, 0)

    def near_first(ring):
        receive(("t", ring, True, 0, 1), block(ring, -1, 0))
        t_send(ring, True, 0, 1)
        receive(("t", ring, False, 1, 1), block(ring, 1, 1))
        t_send(ring, False, 1, 1)

    def near_second(ring):
        receive(("t", ring, True, 1, 1), block(ring, -1, 1))
        receive(("t", ring, False, 0, 1), block(ring, 1, 0))
        to_sibling(ring, -1)
        to_sibling(ring, 1)

    def far(ring):
        receive(("t", ring, True, 0, 2), block(ring, 2, 0))
        receive(("t", ring, False, 1, 2), block(ring, 2, 1))
        to_sibling(ring, 2)

    begin_a(0)
    w_send(3)
    begin_b(0)
    to_sibling(0, 0)

    def across(name, blocks, part, src, dst):
        start, count = blocks
        for d in FAR_FIRST:
            send(
                (name, part, start, d),
                src.at[pl.ds(start, count), part, (z + d) % Z],
                dst.at[part, pl.ds(z * Y + start, count)],
                device(dz=d),
            )
        dst[part, pl.ds(z * Y + start, count)] = src[start:start + count, part, z]

    def across_wait(name, blocks, part, dst):
        start, count = blocks
        for d in FAR_FIRST:
            place = dst.at[part, pl.ds((z - d + Z) % Z * Y + start, count)]
            receive((name, part, start, d), place)

    def transform(source, part):
        spread[...] = source[part].astype(F32).reshape(N1 * CW, N2)
        together = jnp.concatenate(
            [spread[pl.ds(c, N1, stride=CW), :].astype(BF) for c in range(CW)], axis=1
        )
        values = dot(first[...], jnp.concatenate([together, together], axis=0))
        for c in range(CW):
            columns = slice(c * N2, (c + 1) * N2)
            re, im = values[:N1, columns], values[N1:, columns]
            turned = jnp.concatenate(
                [re * twiddle[0] - im * twiddle[1], re * twiddle[1] + im * twiddle[0]], axis=1
            )
            in_halves(c, turned)
        stage[...] = dot(split_rows[...], second[...])

    def in_halves(c, value):
        rows = pl.ds(c * N1, N1)
        top, rest = halves(value)
        split_rows[rows, :2 * N2] = top
        split_rows[rows, 2 * N2:4 * N2] = rest
        split_rows[rows, 4 * N2:] = top

    def filter_second():
        for d in FAR_FIRST:
            receive(("fz", 0, d), filt_z.at[0, (z - d + Z) % Z])
        for d in (2, 1, 3):
            send(("fy", 0, d), filt_z.at[0, :, (y + d) % Y], h_in.at[0, :, y], device(dy=d))
        h_in[0, :, y] = filt_z[0, :, y]

    def filter_last():
        for d in (2, 1, 3):
            receive(("fy", 1, d), filt_z.at[1, :, (y - d + Y) % Y])
        for d in FAR_FIRST:
            send(("fz", 1, d), filt_z.at[1, (z + d) % Z], h_in.at[1, z], device(dz=d))
        h_in[1, z] = filt_z[1, z]

    def filter_transform(part):
        if part == 0:
            for d in (2, 1, 3):
                receive(("fy", 0, d), h_in.at[0, :, (y - d + Y) % Y])
        else:
            for d in FAR_FIRST:
                receive(("fz", 1, d), h_in.at[1, (z - d + Z) % Z])
        transform(h_in, part)
        spec_h[part] = stage[...]

    def filter_send():
        for d in (2, 1, 3):
            send(("fy", 1, d), filt_t.at[1, :, (y + d) % Y], filt_z.at[1, :, y], device(dy=d))
        filt_z[1, :, y] = filt_t[1, :, y]

    def w_next(p):
        for j in range(3):
            columns = pl.ds(j * CH, CH)
            rows = pl.ds(((y + PIECE[p] + Y) % Y) * WR, WR)
            receive(("wy", p, j), wall.at[z, :, rows, columns])
        z_send(0, p, True)
        z_send(0, p, False)

    def z_next(s):
        d, p = s // 4 + 1, s % 4
        receive(("z", True, d, p), w_place(-d, p))
        if d < 3 or p < 2:
            z_send(d, p, True)
        receive(("z", False, d, p), w_place(d, p))
        if d < 3 or p >= 2:
            z_send(d, p, False)

    def total(blocks, rows, offsets):
        left, right = [], []
        for offset in offsets:
            source = (z + offset + Z) % Z
            lanes = pl.ds(pl.multiple_of(source * N2, N2), N2)
            left += [tok[b, rows, lanes] for b in blocks]
            right += [wall[source, b] for b in blocks]
        return acc[rows, :] + dot(jnp.concatenate(left, axis=1), jnp.concatenate(right, axis=0))

    def all_rows(blocks, offsets):
        def rows_of(n, carry):
            rows = pl.ds(pl.multiple_of(n * 2 * ROWS, 2 * ROWS), 2 * ROWS)
            acc[rows, :] = total(blocks, rows, offsets)
            return carry

        lax.fori_loop(0, GROUP // (2 * ROWS), rows_of, 0)

    EARLY = (0, -1, 1, -2, 2)
    LATE = (-3, 3)
    ODD = range(1, 2 * X, 2)

    def from_sibling(ring):
        for step in (-1, 1, 2):
            dy = OFFSET[ring] * (1 - core) + step * core
            dx = OFFSET[ring] * core + step * (1 - core)
            receive(("s", ring, step), t_place(dy + Y, dx + X, other=True))
        step = OFFSET[ring]
        receive(("s", 0, step), t_place(step * (1 - core) + Y, step * core + X, other=True))

    def even_early():
        for ring in (1, 2, 3):
            from_sibling(ring)
        all_rows([(x + OFFSET[ring] + X) % X * 2 for ring in (1, 2, 3)], EARLY)

    def odd_early():
        def rows_of(n, carry):
            rows = pl.ds(pl.multiple_of((y + n + Y - 1) % Y * ROWS, ROWS), ROWS)
            acc[rows, :] = total(ODD, rows, EARLY)
            return carry

        lax.fori_loop(0, 3, rows_of, 0)

    def rest():
        from_sibling(4)
        rows = pl.ds(pl.multiple_of((y + 2) % Y * ROWS, ROWS), ROWS)
        acc[rows, :] = total(ODD, rows, EARLY)
        all_rows([(x + 2) % X * 2], EARLY)
        all_rows(range(2 * X), LATE)

    order = [
        (w_next, 1), (w_next, 2), (near_first, 0), (begin, 1), (w_next, 3), (z_next, 0),
        (near_second, 0), (begin, 2), (begin, 3), (near_first, 1), (z_next, 1), (near_second, 1), (z_next, 2),
        (z_next, 3), (near_first, 2), (far, 0), (begin, 4), (near_second, 2), (z_next, 4),
        (near_first, 3), (z_next, 5), (near_second, 3), (near_first, 4), (z_next, 6),
        (near_second, 4), (filter_send,), (filter_second,), (z_next, 7), (far, 1), (far, 2), (z_next, 8), (far, 3), (z_next, 9),
        (z_next, 10), (even_early,), (z_next, 11), (far, 4), (filter_last,), (odd_early,), (rest,),
    ]
    for event, *values in order:
        event(*values)

    for p in range(4):
        receive(("z", p < 2, 4, p), w_place(4, p))

    mine = pl.ds(pl.multiple_of(y * CH, CH), CH)

    def project(n):
        rounded = total(range(2 * X), pl.ds(n * ROWS, ROWS), (4,)).astype(BF)
        proj[pl.ds(8 + n * ROWS, ROWS), :] = rounded.astype(F32)
        if n == 3:
            halo_out[...] = rounded[ROWS - 16:, :]
            send(("halo",), halo_out, halo_in, device(dz=1))

    def short(start, j):
        columns = slice(j * CH, (j + 1) * CH)
        return sum(
            taps[s, j:j + 1, mine] * proj[pl.ds(8 - s + start, N2), columns] for s in range(3)
        )

    def gate(n):
        values = []
        for start in (n * ROWS, n * ROWS + N2):
            query = short(start, 0)
            values.append(short(start, 1) * short(start, 2))
            at = pl.ds(start - n * ROWS, N2)
            share_out[n, 0, at, :] = query.astype(BF)
            share_out[n, 1, at, :] = (query * (bias[:, mine] * values[-1])).astype(BF)
        sig_t[n] = by_channel(*values)

    BLOCKS = ((2, 2), (0, 2))
    project(3)
    project(2)
    project(1)
    gate(3)
    gate(2)
    for part in range(PARTS):
        across("sz", BLOCKS[0], part, sig_t, x_in)
    project(0)
    gate(1)
    receive(("halo",), halo_in)
    before = halo_in[...].astype(F32)[8:, :]
    proj[:8, :] = jnp.where(z > 0, before, 0.0)
    gate(0)
    for part in range(PARTS):
        across("sz", BLOCKS[1], part, sig_t, x_in)
    for d in (2, 1, 3):
        send(("share", d), share_out.at[(y + d) % Y], share_in.at[y], device(dy=d))
    share_in[y] = share_out[y]
    for part in range(PARTS):
        filter_transform(part)

    for part in range(PARTS):
        for blocks in BLOCKS:
            across_wait("sz", blocks, part, x_in)
        transform(x_in, part)
        for c in range(CW):
            rows = pl.ds(c * N1, N1)
            a_re, a_im = stage[rows, :N2], stage[rows, N2:]
            b_re, b_im = spec_h[part, rows, :N2], spec_h[part, rows, N2:]
            in_halves(
                c, jnp.concatenate([a_re * b_re - a_im * b_im, a_re * b_im + a_im * b_re], axis=1)
            )
        stage[...] = dot(split_rows[...], second_back[...])
        turned = []
        for c in range(CW):
            rows = pl.ds(c * N1, N1)
            re, im = stage[rows, :N2], stage[rows, N2:]
            turned.append(
                jnp.concatenate(
                    [re * twiddle[0] + im * twiddle[1], im * twiddle[0] - re * twiddle[1]], axis=0
                )
            )
        top, rest = halves(jnp.concatenate(turned, axis=1))
        values = dot(first_back[...], jnp.concatenate([top, rest, top], axis=0))
        for c in range(CW):
            spread[pl.ds(c, N1, stride=CW), :] = values[:, c * N2:(c + 1) * N2]
        y_out[part] = spread[...].astype(BF).reshape(Z * Y, 2 * CW, N2)
        for dz in (*FAR_FIRST, 0):
            for dy in (2, 1, 3, 0):
                if dz or dy:
                    to = (z + dz) % Z * Y + (y + dy) % Y
                    send(
                        ("conv", part, dz, dy),
                        y_out.at[part, to],
                        conv_in.at[part, y, z],
                        device(dz=dz, dy=dy),
                    )
        conv_in[part, y, z] = y_out[part, seq]
    for d in (2, 1, 3):
        receive(("share", d), share_in.at[(y - d + Y) % Y])
    for part in range(PARTS):
        for dz in (*FAR_FIRST, 0):
            for dy in (2, 1, 3, 0):
                if dz or dy:
                    place = conv_in.at[part, (y - dy + Y) % Y, (z - dz + Z) % Z]
                    receive(("conv", part, dz, dy), place)

    for quarter in range(Y):
        conv = conv_in[:, quarter].astype(F32).reshape(PARTS * Z, 2, CW, N2)
        columns = slice(quarter * CH, (quarter + 1) * CH)
        for i in range(2):
            rows = slice(i * N2, (i + 1) * N2)
            factor = share_in[quarter, 0, rows, :].astype(F32)
            added = share_in[quarter, 1, rows, :].astype(F32)
            out[rows, columns] = (factor * conv[:, i].reshape(CH, N2).T + added).astype(BF)
    assert len(numbers) == COPIES
    for copy in sent:
        copy.wait_send()


COPIES = 9 + 28 + 30 + 16 + 1 + (3 * 7 + 31 + 3) * PARTS + 3


def on_device(tokens, w_in, taps, filt, bias):
    w_parts = w_in.transpose(0, 2, 1, 3)
    hbm = pl.BlockSpec(memory_space=pltpu.HBM)
    vmem = pl.BlockSpec(memory_space=pltpu.VMEM)
    scratch = [
        pltpu.VMEM((ROWS, Y * CH), F32),
        pltpu.VMEM((3, 3, Y * CH), F32),
        pltpu.VMEM((1, Y * CH), F32),
        *(pltpu.VMEM(t.shape, t.dtype) for t in tables()),
        pltpu.VMEM((2 * X, GROUP, FEAT), BF),
        pltpu.VMEM((Z, 2 * X, Y * WR, 3 * CH), BF),
        pltpu.VMEM((GROUP, 3 * CH), F32),
        pltpu.VMEM((GROUP + 8, 3 * CH), F32),
        pltpu.VMEM((16, 3 * CH), BF),
        pltpu.VMEM((16, 3 * CH), BF),
        pltpu.VMEM((Y, 2, ROWS, CH), BF),
        pltpu.VMEM((Y, 2, ROWS, CH), BF),
        pltpu.VMEM((Y, PARTS, Z, 2 * CW, N2), BF),
        pltpu.VMEM((PARTS, Y, Z, 2 * CW, N2), BF),
        pltpu.VMEM((PARTS, Z, Y, 2 * CW, N2), BF),
        pltpu.VMEM((PARTS, Z, Y, 2 * CW, N2), BF),
        pltpu.VMEM((PARTS, Z * Y, 2 * CW, N2), BF),
        pltpu.VMEM((PARTS, Z, Y, 2 * CW, N2), BF),
        pltpu.VMEM((N1 * CW, N2), F32),
        pltpu.VMEM((CW * N1, 2 * N2), F32),
        pltpu.VMEM((CW * N1, 6 * N2), BF),
        pltpu.VMEM((PARTS, CW * N1, 2 * N2), F32),
        pltpu.VMEM((PARTS, Z * Y, 2 * CW, N2), BF),
        pltpu.SemaphoreType.DMA((COPIES,)),
        pltpu.SemaphoreType.DMA((COPIES,)),
        pltpu.SemaphoreType.DMA((12,)),
    ]
    return pl.pallas_call(
        kernel,
        out_shape=jax.ShapeDtypeStruct((ROWS, Y * CH), BF),
        in_specs=[hbm] * 10,
        out_specs=vmem,
        scratch_shapes=scratch,
        compiler_params=pltpu.CompilerParams(
            collective_id=0, has_side_effects=True, vmem_limit_bytes=60 * 1024 * 1024
        ),
        name="layer",
    )(tokens, w_parts, filt, taps, bias[None, :], *(jnp.asarray(t) for t in tables()))


def solution(mesh):
    return jax.shard_map(
        on_device,
        mesh=mesh,
        in_specs=(
            P("seq", "ch"),
            P(None, "seq", None, "ch"),
            P(None, None, "ch"),
            P("seq", "ch"),
            P("ch"),
        ),
        out_specs=P("seq", "ch"),
        check_vma=False,
    )
```

```python
import functools

import jax
import jax.numpy as jnp
import ml_dtypes
import numpy as np
from jax import lax
from jax.experimental import pallas as pl
from jax.experimental.pallas import tpu as pltpu
from jax.sharding import PartitionSpec as P

MESH = pl.DeviceIdType.MESH
BF = jnp.bfloat16
F32 = jnp.float32

Z, Y, X = 8, 4, 4
ROWS = 256
FEAT = 1024
GROUP = Y * ROWS
CH = 128
PARTS = 2
CW = CH // Z // PARTS
WR = 32
N1, N2 = 64, 128
POINTS = N1 * N2
THETA = 0.25
FAR_FIRST = (4, 3, 5, 2, 6, 1, 7)
PIECE = (0, -1, 1, 2)


def split(value):
    high = value.astype(ml_dtypes.bfloat16)
    low = (value - high.astype(np.float64)).astype(ml_dtypes.bfloat16)
    return np.stack([high, low])


@functools.cache
def tables():
    k1 = np.arange(N1)[:, None] + THETA
    angle = 2 * np.pi * k1 * np.arange(N1)[None, :] / N1
    first = np.concatenate([np.cos(angle), -np.sin(angle)], axis=0)
    angle = 2 * np.pi * k1 * np.arange(N2)[None, :] / POINTS
    twiddle = np.stack([np.cos(angle), -np.sin(angle)]).astype(np.float32)
    angle = 2 * np.pi * (np.arange(N2)[:, None] * np.arange(N2)[None, :] % N2) / N2
    cos, sin = np.cos(angle), np.sin(angle)
    second = split(np.block([[cos, -sin], [sin, cos]]))
    second_back = split(np.block([[cos, sin], [-sin, cos]]))
    first_back = split(first.T / POINTS)
    return (
        np.concatenate(list(split(first)), axis=1),
        np.concatenate([first_back[0], first_back[0], first_back[1]], axis=1),
        twiddle,
        np.concatenate([second[0], second[0], second[1]], axis=0),
        np.concatenate([second_back[0], second_back[0], second_back[1]], axis=0),
    )


def dot(a, b):
    return jnp.dot(a, b, preferred_element_type=F32)


def halves(value):
    high = value.astype(BF)
    return high, (value - high.astype(F32)).astype(BF)


def by_channel(even, odd):
    turned = [value.T.reshape(CH // CW, CW, N2) for value in (even, odd)]
    return jnp.concatenate(turned, axis=1).astype(BF).reshape(PARTS, Z, 2 * CW, N2)


def kernel(
    tok_in, w_in, filt_in, taps_in, bias_in, first_in, first_back_in, twiddle_in, second_in,
    second_back_in, out,
    filt, taps, bias, first, first_back, twiddle, second, second_back, tok, wall, acc, proj, halo_out, halo_in, share_out, share_in, sig_t, conv_in,
    filt_t, filt_z, x_in, h_in, spread, stage, split_rows, spec_h, y_out,
    send_sem, recv_sem, local_sem,
):
    seq, ch = lax.axis_index("seq"), lax.axis_index("ch")
    z, y, x, core = seq // Y, seq % Y, ch // 2, ch % 2
    numbers = {}

    def number(key):
        return numbers.setdefault(key, len(numbers))

    def device(dz=0, dy=0, dx=0, flip=False):
        to_seq = ((z + dz + Z) % Z) * Y + (y + dy + Y) % Y
        to_ch = ((x + dx + X) % X) * 2 + (1 - core if flip else core)
        return (to_seq, to_ch)

    def remote(key, src, dst, target):
        n = number(key)
        return pltpu.make_async_remote_copy(
            src_ref=src, dst_ref=dst, send_sem=send_sem.at[n], recv_sem=recv_sem.at[n],
            device_id=target, device_id_type=MESH,
        )

    sent = []

    def send(key, src, dst, target):
        copy = remote(key, src, dst, target)
        copy.start()
        sent.append(copy)

    def sent_all(count=None):
        for copy in sent[:count]:
            copy.wait_send()
        del sent[:count]

    def receive(key, dst):
        remote(key, dst, dst, device(flip=True)).wait_recv()

    def w_place(dz, p):
        return wall.at[(z + dz + Z) % Z, :, pl.ds(((y + PIECE[p] + Y) % Y) * WR, WR), :]

    def t_place(dy, dx, other=False, half=None):
        b = ((x + dx + X) % X) * 2 + (1 - core if other else core)
        start = ((y + dy + Y) % Y) * ROWS
        if half is None:
            return tok.at[b, pl.ds(start, ROWS), :]
        return tok.at[b, pl.ds(start + half * (ROWS // 2), ROWS // 2), :]

    def along(axis, step):
        on_x = (1 - core) if axis == 0 else core
        return step * (1 - on_x), step * on_x

    def shift(axis, step):
        dy, dx = along(axis, step)
        return device(dy=dy, dx=dx)

    peers = [device(dz=dz, dy=dy) for dz in range(Z) for dy in range(Y) if dz or dy]
    peers += [device(dx=1), device(dx=-1), device(flip=True)]
    barrier = pltpu.get_barrier_semaphore()
    for peer in peers:
        pl.semaphore_signal(barrier, inc=1, device_id=peer, device_id_type=MESH)

    own_tok = pltpu.make_async_copy(tok_in, t_place(0, 0), local_sem.at[0])
    def w_columns(to, j):
        return w_in.at[:, j, :, pl.ds(to * CH, CH)]

    def w_home(j):
        return wall.at[z, :, pl.ds(y * WR, WR), pl.ds(j * CH, CH)]

    own_w = [pltpu.make_async_copy(w_columns(y, j), w_home(j), local_sem.at[1 + j]) for j in range(3)]
    pairs = [(filt_in, filt), (taps_in, taps), (bias_in, bias), (first_in, first), (first_back_in, first_back)]
    pairs += [(twiddle_in, twiddle), (second_in, second), (second_back_in, second_back)]
    own = [pltpu.make_async_copy(a, b, local_sem.at[4 + n]) for n, (a, b) in enumerate(pairs)]
    for copy in own[:1] + own_w + [own_tok] + own[1:]:
        copy.start()

    own[0].wait()
    for quarter in range(Y):
        columns = slice(quarter * CH, (quarter + 1) * CH)
        filt_t[:, :, quarter] = by_channel(filt[:N2, columns], filt[N2:, columns])
    acc[...] = jnp.zeros_like(acc)

    pl.semaphore_wait(barrier, len(peers))

    for copy in own_w:
        copy.wait()

    def z_send(d, p, right):
        step = 1 if right else -1
        place = w_place(-step * d, p)
        send(("z", right, d + 1, p), place, place, device(dz=step))

    def w_send(p):
        to = -PIECE[p]
        for j in range(3):
            send(("wy", p, j), w_columns((y + to + Y) % Y, j), w_home(j), device(dy=to))

    z_send(0, 0, True)
    z_send(0, 0, False)
    w_send(1)
    w_send(2)
    for d in FAR_FIRST:
        send(("fz", 0, d), filt_t.at[0, (z + d) % Z], filt_z.at[0, z], device(dz=d))
    filt_z[0, z] = filt_t[0, z]
    own_tok.wait()
    for copy in own[1:]:
        copy.wait()

    OFFSET = (0, 0, 1, -1, 2)

    def block(ring, step, half=None):
        if ring == 0:
            dy, dx = along(0, step)
        else:
            ay, ax = along(0, OFFSET[ring])
            by, bx = along(1, step)
            dy, dx = ay + by, ax + bx
        return t_place(dy + Y, dx + X, half=half)

    def t_send(ring, right, half, d):
        step = 1 if right else -1
        place = block(ring, -step * d, half)
        send(("t", ring, right, half, d + 1), place, place, shift(0 if ring == 0 else 1, step))

    def to_sibling(ring, step):
        place = block(ring, step)
        send(("s", ring, step), place, place, device(flip=True))

    def begin(ring):
        t_send(ring, True, 0, 0)
        t_send(ring, False, 1, 0)
        t_send(ring, True, 1, 0)
        t_send(ring, False, 0, 0)

    def begin_a(ring):
        t_send(ring, True, 0, 0)
        t_send(ring, False, 1, 0)

    def begin_b(ring):
        t_send(ring, True, 1, 0)
        t_send(ring, False, 0, 0)

    def near_first(ring):
        receive(("t", ring, True, 0, 1), block(ring, -1, 0))
        t_send(ring, True, 0, 1)
        receive(("t", ring, False, 1, 1), block(ring, 1, 1))
        t_send(ring, False, 1, 1)

    def near_second(ring):
        receive(("t", ring, True, 1, 1), block(ring, -1, 1))
        receive(("t", ring, False, 0, 1), block(ring, 1, 0))
        to_sibling(ring, -1)
        to_sibling(ring, 1)

    def far(ring):
        receive(("t", ring, True, 0, 2), block(ring, 2, 0))
        receive(("t", ring, False, 1, 2), block(ring, 2, 1))
        to_sibling(ring, 2)

    begin_a(0)
    w_send(3)
    begin_b(0)
    to_sibling(0, 0)

    def across(name, blocks, part, src, dst):
        start, count = blocks
        for d in FAR_FIRST:
            send(
                (name, part, start, d),
                src.at[pl.ds(start, count), part, (z + d) % Z],
                dst.at[part, pl.ds(z * Y + start, count)],
                device(dz=d),
            )
        dst[part, pl.ds(z * Y + start, count)] = src[start:start + count, part, z]

    def across_wait(name, blocks, part, dst):
        start, count = blocks
        for d in FAR_FIRST:
            place = dst.at[part, pl.ds((z - d + Z) % Z * Y + start, count)]
            receive((name, part, start, d), place)

    def transform(source, part):
        spread[...] = source[part].astype(F32).reshape(N1 * CW, N2)
        together = jnp.concatenate(
            [spread[pl.ds(c, N1, stride=CW), :].astype(BF) for c in range(CW)], axis=1
        )
        values = dot(first[...], jnp.concatenate([together, together], axis=0))
        for c in range(CW):
            columns = slice(c * N2, (c + 1) * N2)
            re, im = values[:N1, columns], values[N1:, columns]
            turned = jnp.concatenate(
                [re * twiddle[0] - im * twiddle[1], re * twiddle[1] + im * twiddle[0]], axis=1
            )
            in_halves(c, turned)
        stage[...] = dot(split_rows[...], second[...])

    def in_halves(c, value):
        rows = pl.ds(c * N1, N1)
        top, rest = halves(value)
        split_rows[rows, :2 * N2] = top
        split_rows[rows, 2 * N2:4 * N2] = rest
        split_rows[rows, 4 * N2:] = top

    def filter_second():
        for d in FAR_FIRST:
            receive(("fz", 0, d), filt_z.at[0, (z - d + Z) % Z])
        for d in (2, 1, 3):
            send(("fy", 0, d), filt_z.at[0, :, (y + d) % Y], h_in.at[0, :, y], device(dy=d))
        h_in[0, :, y] = filt_z[0, :, y]

    def filter_last():
        for d in (2, 1, 3):
            receive(("fy", 1, d), filt_z.at[1, :, (y - d + Y) % Y])
        for d in FAR_FIRST:
            send(("fz", 1, d), filt_z.at[1, (z + d) % Z], h_in.at[1, z], device(dz=d))
        h_in[1, z] = filt_z[1, z]

    def filter_transform(part):
        if part == 0:
            for d in (2, 1, 3):
                receive(("fy", 0, d), h_in.at[0, :, (y - d + Y) % Y])
        else:
            for d in FAR_FIRST:
                receive(("fz", 1, d), h_in.at[1, (z - d + Z) % Z])
        transform(h_in, part)
        spec_h[part] = stage[...]

    def filter_send():
        for d in (2, 1, 3):
            send(("fy", 1, d), filt_t.at[1, :, (y + d) % Y], filt_z.at[1, :, y], device(dy=d))
        filt_z[1, :, y] = filt_t[1, :, y]

    def w_next(p):
        for j in range(3):
            columns = pl.ds(j * CH, CH)
            rows = pl.ds(((y + PIECE[p] + Y) % Y) * WR, WR)
            receive(("wy", p, j), wall.at[z, :, rows, columns])
        z_send(0, p, True)
        z_send(0, p, False)

    def z_next(s):
        d, p = s // 4 + 1, s % 4
        receive(("z", True, d, p), w_place(-d, p))
        if d < 3 or p < 2:
            z_send(d, p, True)
        receive(("z", False, d, p), w_place(d, p))
        if d < 3 or p >= 2:
            z_send(d, p, False)

    def total(blocks, rows, offsets):
        left, right = [], []
        for offset in offsets:
            source = (z + offset + Z) % Z
            lanes = pl.ds(pl.multiple_of(source * N2, N2), N2)
            left += [tok[b, rows, lanes] for b in blocks]
            right += [wall[source, b] for b in blocks]
        return acc[rows, :] + dot(jnp.concatenate(left, axis=1), jnp.concatenate(right, axis=0))

    def all_rows(blocks, offsets):
        def rows_of(n, carry):
            rows = pl.ds(pl.multiple_of(n * 2 * ROWS, 2 * ROWS), 2 * ROWS)
            acc[rows, :] = total(blocks, rows, offsets)
            return carry

        lax.fori_loop(0, GROUP // (2 * ROWS), rows_of, 0)

    EARLY = (0, -1, 1, -2, 2)
    LATE = (-3, 3)
    ODD = range(1, 2 * X, 2)

    def from_sibling(ring):
        for step in (-1, 1, 2):
            dy = OFFSET[ring] * (1 - core) + step * core
            dx = OFFSET[ring] * core + step * (1 - core)
            receive(("s", ring, step), t_place(dy + Y, dx + X, other=True))
        step = OFFSET[ring]
        receive(("s", 0, step), t_place(step * (1 - core) + Y, step * core + X, other=True))

    def even_early():
        for ring in (1, 2, 3):
            from_sibling(ring)
        all_rows([(x + OFFSET[ring] + X) % X * 2 for ring in (1, 2, 3)], EARLY)

    def odd_early():
        def rows_of(n, carry):
            rows = pl.ds(pl.multiple_of((y + n + Y - 1) % Y * ROWS, ROWS), ROWS)
            acc[rows, :] = total(ODD, rows, EARLY)
            return carry

        lax.fori_loop(0, 3, rows_of, 0)

    def rest():
        from_sibling(4)
        rows = pl.ds(pl.multiple_of((y + 2) % Y * ROWS, ROWS), ROWS)
        acc[rows, :] = total(ODD, rows, EARLY)
        all_rows([(x + 2) % X * 2], EARLY)
        all_rows(range(2 * X), LATE)

    order = [
        (w_next, 1), (w_next, 2), (near_first, 0), (begin, 1), (w_next, 3), (z_next, 0),
        (near_second, 0), (begin, 2), (begin, 3), (near_first, 1), (z_next, 1), (near_second, 1), (z_next, 2),
        (z_next, 3), (near_first, 2), (far, 0), (begin, 4), (near_second, 2), (z_next, 4),
        (near_first, 3), (z_next, 5), (near_second, 3), (near_first, 4), (z_next, 6),
        (near_second, 4), (filter_send,), (filter_second,), (z_next, 7), (far, 1), (far, 2), (z_next, 8), (far, 3), (z_next, 9),
        (z_next, 10), (even_early,), (z_next, 11), (far, 4), (filter_last,), (odd_early,), (rest,),
    ]
    for event, *values in order:
        event(*values)

    for p in range(4):
        receive(("z", p < 2, 4, p), w_place(4, p))

    mine = pl.ds(pl.multiple_of(y * CH, CH), CH)

    ring_copies = len(sent)

    def project(n):
        rounded = total(range(2 * X), pl.ds(n * ROWS, ROWS), (4,)).astype(BF)
        proj[pl.ds(8 + n * ROWS, ROWS), :] = rounded.astype(F32)
        if n == 3:
            halo_out[...] = rounded[ROWS - 16:, :]
            send(("halo",), halo_out, halo_in, device(dz=1))

    def short(start, j):
        columns = slice(j * CH, (j + 1) * CH)
        return sum(
            taps[s, j:j + 1, mine] * proj[pl.ds(8 - s + start, N2), columns] for s in range(3)
        )

    def gate(n):
        values = []
        for start in (n * ROWS, n * ROWS + N2):
            query = short(start, 0)
            values.append(short(start, 1) * short(start, 2))
            at = pl.ds(start - n * ROWS, N2)
            share_out[n, 0, at, :] = query.astype(BF)
            share_out[n, 1, at, :] = (query * (bias[:, mine] * values[-1])).astype(BF)
        sig_t[n] = by_channel(*values)

    BLOCKS = ((2, 2), (0, 2))
    project(3)
    project(2)
    project(1)
    gate(3)
    gate(2)
    for part in range(PARTS):
        across("sz", BLOCKS[0], part, sig_t, x_in)
    project(0)
    gate(1)
    receive(("halo",), halo_in)
    before = halo_in[...].astype(F32)[8:, :]
    proj[:8, :] = jnp.where(z > 0, before, 0.0)
    gate(0)
    for part in range(PARTS):
        across("sz", BLOCKS[1], part, sig_t, x_in)
    for d in (2, 1, 3):
        send(("share", d), share_out.at[(y + d) % Y], share_in.at[y], device(dy=d))
    share_in[y] = share_out[y]
    for part in range(PARTS):
        filter_transform(part)
    sent_all(ring_copies)

    for part in range(PARTS):
        for blocks in BLOCKS:
            across_wait("sz", blocks, part, x_in)
        transform(x_in, part)
        for c in range(CW):
            rows = pl.ds(c * N1, N1)
            a_re, a_im = stage[rows, :N2], stage[rows, N2:]
            b_re, b_im = spec_h[part, rows, :N2], spec_h[part, rows, N2:]
            in_halves(
                c, jnp.concatenate([a_re * b_re - a_im * b_im, a_re * b_im + a_im * b_re], axis=1)
            )
        stage[...] = dot(split_rows[...], second_back[...])
        turned = []
        for c in range(CW):
            rows = pl.ds(c * N1, N1)
            re, im = stage[rows, :N2], stage[rows, N2:]
            turned.append(
                jnp.concatenate(
                    [re * twiddle[0] + im * twiddle[1], im * twiddle[0] - re * twiddle[1]], axis=0
                )
            )
        top, rest = halves(jnp.concatenate(turned, axis=1))
        values = dot(first_back[...], jnp.concatenate([top, rest, top], axis=0))
        for c in range(CW):
            spread[pl.ds(c, N1, stride=CW), :] = values[:, c * N2:(c + 1) * N2]
        y_out[part] = spread[...].astype(BF).reshape(Z * Y, 2 * CW, N2)
        for dz in (*FAR_FIRST, 0):
            for dy in (2, 1, 3, 0):
                if dz or dy:
                    to = (z + dz) % Z * Y + (y + dy) % Y
                    send(
                        ("conv", part, dz, dy),
                        y_out.at[part, to],
                        conv_in.at[part, y, z],
                        device(dz=dz, dy=dy),
                    )
        conv_in[part, y, z] = y_out[part, seq]
    sent_all()
    for d in (2, 1, 3):
        receive(("share", d), share_in.at[(y - d + Y) % Y])
    for part in range(PARTS):
        for dz in (*FAR_FIRST, 0):
            for dy in (2, 1, 3, 0):
                if dz or dy:
                    place = conv_in.at[part, (y - dy + Y) % Y, (z - dz + Z) % Z]
                    receive(("conv", part, dz, dy), place)

    for quarter in range(Y):
        conv = conv_in[:, quarter].astype(F32).reshape(PARTS * Z, 2, CW, N2)
        columns = slice(quarter * CH, (quarter + 1) * CH)
        for i in range(2):
            rows = slice(i * N2, (i + 1) * N2)
            factor = share_in[quarter, 0, rows, :].astype(F32)
            added = share_in[quarter, 1, rows, :].astype(F32)
            out[rows, columns] = (factor * conv[:, i].reshape(CH, N2).T + added).astype(BF)
    assert len(numbers) == COPIES


COPIES = 9 + 28 + 30 + 16 + 1 + (3 * 7 + 31 + 3) * PARTS + 3


def on_device(tokens, w_in, taps, filt, bias):
    w_parts = w_in.transpose(0, 2, 1, 3)
    hbm = pl.BlockSpec(memory_space=pltpu.HBM)
    vmem = pl.BlockSpec(memory_space=pltpu.VMEM)
    scratch = [
        pltpu.VMEM((ROWS, Y * CH), F32),
        pltpu.VMEM((3, 3, Y * CH), F32),
        pltpu.VMEM((1, Y * CH), F32),
        *(pltpu.VMEM(t.shape, t.dtype) for t in tables()),
        pltpu.VMEM((2 * X, GROUP, FEAT), BF),
        pltpu.VMEM((Z, 2 * X, Y * WR, 3 * CH), BF),
        pltpu.VMEM((GROUP, 3 * CH), F32),
        pltpu.VMEM((GROUP + 8, 3 * CH), F32),
        pltpu.VMEM((16, 3 * CH), BF),
        pltpu.VMEM((16, 3 * CH), BF),
        pltpu.VMEM((Y, 2, ROWS, CH), BF),
        pltpu.VMEM((Y, 2, ROWS, CH), BF),
        pltpu.VMEM((Y, PARTS, Z, 2 * CW, N2), BF),
        pltpu.VMEM((PARTS, Y, Z, 2 * CW, N2), BF),
        pltpu.VMEM((PARTS, Z, Y, 2 * CW, N2), BF),
        pltpu.VMEM((PARTS, Z, Y, 2 * CW, N2), BF),
        pltpu.VMEM((PARTS, Z * Y, 2 * CW, N2), BF),
        pltpu.VMEM((PARTS, Z, Y, 2 * CW, N2), BF),
        pltpu.VMEM((N1 * CW, N2), F32),
        pltpu.VMEM((CW * N1, 2 * N2), F32),
        pltpu.VMEM((CW * N1, 6 * N2), BF),
        pltpu.VMEM((PARTS, CW * N1, 2 * N2), F32),
        pltpu.VMEM((PARTS, Z * Y, 2 * CW, N2), BF),
        pltpu.SemaphoreType.DMA((COPIES,)),
        pltpu.SemaphoreType.DMA((COPIES,)),
        pltpu.SemaphoreType.DMA((12,)),
    ]
    return pl.pallas_call(
        kernel,
        out_shape=jax.ShapeDtypeStruct((ROWS, Y * CH), BF),
        in_specs=[hbm] * 10,
        out_specs=vmem,
        scratch_shapes=scratch,
        compiler_params=pltpu.CompilerParams(
            collective_id=0, has_side_effects=True, vmem_limit_bytes=60 * 1024 * 1024
        ),
        name="layer",
    )(tokens, w_parts, filt, taps, bias[None, :], *(jnp.asarray(t) for t in tables()))


def solution(mesh):
    return jax.shard_map(
        on_device,
        mesh=mesh,
        in_specs=(
            P("seq", "ch"),
            P(None, "seq", None, "ch"),
            P(None, None, "ch"),
            P("seq", "ch"),
            P("ch"),
        ),
        out_specs=P("seq", "ch"),
        check_vma=False,
    )
```
